32 devices in a mesh: groups: 2 (over y), blk: 4 (over x, core), rep: 4 (over z).
Axes of the slice: x: 2, y: 2, z: 4, core: 2. Of those that a mesh axis runs over, the one named last changes fastest.
Arguments:
- features: bfloat16 [8192, 256], P(('groups', 'blk')), parts along dimension 0, may hold values from -6 to 6
- weight: bfloat16 [256, 256], replicated, may hold values from -0.375 to 0.375
- cotangent: bfloat16 [8192, 256], P(('groups', 'blk', 'rep')), parts along dimension 0, may hold values from -6 to 6
- tiles: bfloat16 [8, 4, 4, 2, 256, 256], P(('groups', 'blk'), 'rep'), parts along dimension 0, may hold values from -0.1875 to 0.1875
- tile_rows: int32 [8, 4, 4, 2], P(('groups', 'blk'), 'rep'), parts along dimension 0, may hold values from 0 to 3, as said below
- tile_cols: int32 [8, 4, 4, 2], P(('groups', 'blk'), 'rep'), parts along dimension 0, may hold values from 0 to 3
- tile_count: int32 [8, 4, 4], P(('groups', 'blk'), 'rep'), parts along dimension 0, may hold values from 0 to 2, as said below
Outputs:
- output: bfloat16 [8192, 256], P(('groups', 'blk', 'rep')), parts along dimension 0
- feature_grad: bfloat16 [8192, 256], P(('groups', 'blk', 'rep')), parts along dimension 0
- weight_grad: float32 [512, 256], P('groups'), parts along dimension 0
The draws below stay inside these ranges and needn't reach their ends.
There are 2 independent parts, one for each index of `groups`. The reference program is written for one: setup_inputs(seed, part) draws one part's arguments, and reference() takes and returns one part's arrays. A program takes and returns all parts, laid end to end along the dimension named above; an argument that names none is the same for every part. Nothing has to cross between parts.
Inputs may be any that keep to these rules, and one draw needn't show every extreme that they name: `tile_count`: an owner reaches its own panels and those of its two neighbours along the loop from every device along rep, and uses all 2 slots on its own panels; any other owner is reached by all devices along rep or by none, and for every distance along the loop some owner reaches the owner that far away. `tile_rows`: for one row owner and one source owner, the slots of all devices along rep name distinct (row panel, column panel) pairs.
All inputs are finite; a program needn't handle non-finite values.
Results may differ from the reference program's by a relative error of at most 0.0065.
Values may be sent and summed in bfloat16 or wider, within the bound.
A program may use at most 64 MiB of HBM per device.

```python
import jax
import jax.numpy as jnp
from jax import lax

D = 256
TILE = 256
PAN_BLK = 4
SLOTS = 2
NODES = 4096
N_BLK = 4
N_REP = 4


def positions(key):
    base = jax.random.fold_in(key, 11)
    pair_keys = jax.random.split(base, N_BLK * N_BLK)
    orders = jax.vmap(lambda one_key: jax.random.permutation(one_key, PAN_BLK * PAN_BLK))(pair_keys)
    taken = orders[:, :N_REP * SLOTS].reshape(N_BLK, N_BLK, N_REP, SLOTS)
    return jnp.transpose(taken, (0, 2, 1, 3)).astype(jnp.int32)


def draw_tile_rows(key, part):
    shared = positions(key)
    return (shared // PAN_BLK).astype(jnp.int32)


def draw_tile_cols(key, part):
    shared = positions(key)
    return (shared % PAN_BLK).astype(jnp.int32)


def draw_tile_count(key, part):
    key = jax.random.fold_in(key, 7)
    first_key, second_key, third_key = jax.random.split(key, 3)
    owner = jnp.arange(N_BLK, dtype=jnp.int32)
    distance = jnp.mod(owner[:, None] - owner[None, :], N_BLK)
    band = (distance == 0) | (distance == 1) | (distance == N_BLK - 1)
    extra = jax.random.randint(first_key, (N_BLK, N_BLK), 0, 3) == 0
    picked_row = jax.random.randint(second_key, (N_BLK,), 0, N_BLK)
    forced = owner[:, None] == picked_row[distance]
    reached = band | extra | forced
    counts = jax.random.randint(third_key, (N_BLK, N_REP, N_BLK), 1, SLOTS + 1)
    counts = jnp.where(distance[:, None, :] == 0, SLOTS, counts)
    return jnp.where(reached[:, None, :], counts, 0).astype(jnp.int32)


def level_of(own_key, dims, cuts, least, largest):
    level, own = 1.0, jax.random.fold_in(own_key, 6)
    for axis_at, blocks in cuts:
        draws = jnp.exp(jax.random.uniform(jax.random.fold_in(own, axis_at), (blocks,), jnp.float32, least / len(cuts), largest / len(cuts)))
        level = level * jnp.repeat(draws, dims[axis_at] // blocks).reshape([-1 if axis == axis_at else 1 for axis in range(len(dims))])
    return level


def gaussian(rng, dims, scale, most, cuts=(), held_as=jnp.bfloat16):
    drawn = scale * jax.random.normal(rng, dims, jnp.float32)
    if cuts:
        drawn = drawn * level_of(rng, dims, cuts, -0.22, 0.18)
    return jnp.clip(drawn, -most, most).astype(held_as)


def setup_inputs(seed: int = 0, part: int = 0) -> dict:
    keys = jax.random.split(jax.random.key(seed), 8)
    part_keys = jax.random.split(jax.random.fold_in(keys[7], part), 8)
    return {
        "features": gaussian(part_keys[0], (NODES, D), 1.0, 6.0, ((0, 4),)),
        "weight": gaussian(keys[1], (D, D), D ** -0.5, 0.375),
        "cotangent": gaussian(part_keys[2], (NODES, D), 1.0, 6.0, ((0, 16),)),
        "tiles": gaussian(part_keys[3], (N_BLK, N_REP, N_BLK, SLOTS, TILE, TILE), (N_BLK * N_REP * SLOTS * TILE // (2 * PAN_BLK)) ** -0.5, 0.1875, ((0, 4), (1, 4))),
        "tile_rows": draw_tile_rows(jax.random.fold_in(jax.random.fold_in(keys[7], part), 71), part),
        "tile_cols": draw_tile_cols(jax.random.fold_in(jax.random.fold_in(keys[7], part), 71), part),
        "tile_count": draw_tile_count(jax.random.fold_in(jax.random.fold_in(keys[7], part), 71), part),
    }


def activation(values):
    return jax.nn.gelu(values, approximate=True)

def reference(features, weight, cotangent, tiles, tile_rows, tile_cols, tile_count):
    hidden = features.shape[1]
    tile_size = tiles.shape[-1]
    owner_total = tiles.shape[0]
    slot_total = tiles.shape[3]
    panel_count = features.shape[0] // tile_size
    feat_panels = features.astype(jnp.float32).reshape(panel_count, tile_size, hidden)
    slot_ids = jnp.arange(slot_total, dtype=jnp.int32)
    owner_ids = jnp.arange(owner_total, dtype=jnp.int32)
    col_global = (owner_ids[None, None, :, None] * PAN_BLK + tile_cols).astype(jnp.int32)
    row_global = (owner_ids[:, None, None, None] * PAN_BLK + tile_rows).astype(jnp.int32)
    active = (slot_ids[None, None, None, :] < tile_count[..., None]).astype(jnp.float32)

    def forward_block(carry_value, inputs):
        tile_blocks, rows_local, cols_glob, alive_mask = inputs
        chosen = feat_panels[cols_glob]
        product = jnp.einsum('rosij,rosjd->rosid', tile_blocks.astype(jnp.float32), chosen)
        product = product * alive_mask[..., None, None]
        panel_out = jnp.zeros((PAN_BLK, tile_size, hidden), jnp.float32).at[rows_local].add(product)
        return (carry_value, panel_out)
    _, aggregated_f = lax.scan(forward_block, jnp.zeros((), jnp.float32), (tiles, tile_rows, col_global, active))
    aggregated = aggregated_f.reshape(-1, hidden).astype(jnp.bfloat16)
    pre_act = jnp.dot(aggregated, weight, preferred_element_type=jnp.float32)
    output_vals, gelu_back = jax.vjp(activation, pre_act)
    output = output_vals.astype(jnp.bfloat16)
    pre_grad = gelu_back(cotangent.astype(jnp.float32))[0].astype(jnp.bfloat16)
    weight_grad = jnp.dot(aggregated.T, pre_grad, preferred_element_type=jnp.float32)
    agg_grad = jnp.dot(pre_grad, weight.T, preferred_element_type=jnp.float32).astype(jnp.bfloat16)
    grad_panels = agg_grad.astype(jnp.float32).reshape(panel_count, tile_size, hidden)

    def backward_block(running, inputs):
        tile_blocks, rows_glob, cols_glob, alive_mask = inputs
        chosen = grad_panels[rows_glob]
        product = jnp.einsum('rosij,rosid->rosjd', tile_blocks.astype(jnp.float32), chosen)
        product = product * alive_mask[..., None, None]
        return (running.at[cols_glob].add(product), jnp.zeros((), jnp.float32))
    initial = jnp.zeros((panel_count, tile_size, hidden), jnp.float32)
    feature_total, _ = lax.scan(backward_block, initial, (tiles, row_global, col_global, active))
    feature_grad = feature_total.reshape(-1, hidden).astype(jnp.bfloat16)
    return (output, feature_grad, weight_grad)
```

```python
import functools

import jax
import jax.numpy as jnp
from jax import lax
from jax.experimental import pallas as pl
from jax.experimental.pallas import tpu as pltpu
from jax.sharding import PartitionSpec as P

MESH = pl.DeviceIdType.MESH
HALVES = 2
F32 = jnp.float32
BF16 = jnp.bfloat16
GELU_SCALE = 0.7978845608028654
GELU_CUBIC = 0.044715


def dot(left, right, left_dim, right_dim):
    return lax.dot_general(
        left, right, (((left_dim,), (right_dim,)), ((), ())), preferred_element_type=F32
    )


def layer_kernel(
    n_blk, n_rep,
    feat, weight, cot, tiles, rows, cols, count, cols_vec,
    out, fgrad, wgrad,
    idx_vec, idx, fsend, frecv, acc, rsend, rrecv, agg, grad0, grad1,
    bsend, brecv, facc, qsend, qrecv, wlocal, wrecv, wrep,
    idx_send, idx_recv, idx_local, f_send, f_recv, r_send, r_recv, g_send, g_recv,
    b_send, b_recv, q_send, q_recv, w1_send, w1_recv, w2_send, w2_recv, w3_send, w3_recv,
):
    tile = tiles.shape[-1]
    slots = tiles.shape[1]
    panels = feat.shape[0]
    hidden = feat.shape[2]
    width = hidden // HALVES
    chunk = panels * tile // n_rep
    per_panel = tile // chunk
    wchunk = hidden // n_blk
    chips = n_blk // 2
    blk = lax.axis_index("blk")
    rep = lax.axis_index("rep")
    chip, core = blk // 2, blk % 2
    grads = (grad0, grad1)

    def blk_to(j):
        return ((chip + j // 2) % chips) * 2 + (core + j) % 2

    def blk_from(j):
        return ((chip + chips - j // 2) % chips) * 2 + (core + j) % 2

    def rep_to(k):
        return (rep + k) % n_rep

    def to_blk(j, src, dst, send_sem, recv_sem):
        return pltpu.make_async_remote_copy(
            src_ref=src, dst_ref=dst, send_sem=send_sem, recv_sem=recv_sem,
            device_id={"blk": blk_to(j)}, device_id_type=MESH,
        )

    def to_rep(k, src, dst, send_sem, recv_sem):
        return pltpu.make_async_remote_copy(
            src_ref=src, dst_ref=dst, send_sem=send_sem, recv_sem=recv_sem,
            device_id={"rep": rep_to(k)}, device_id_type=MESH,
        )

    def each(total, body):
        def step(at, carry):
            body(at)
            return carry
        if total <= 4:
            for at in range(1, total):
                body(at)
        else:
            lax.fori_loop(1, total, step, 0)

    def far_first(body):
        if n_blk <= 4:
            for j in list(range(2, n_blk)) + [1]:
                body(j)
        else:
            each(n_blk, body)

    my_part = pl.ds(pl.multiple_of((rep % per_panel) * chunk, chunk), chunk)

    def idx_copy(j):
        return to_blk(j, cols_vec, idx_vec.at[j], idx_send.at[j], idx_recv.at[j])

    def feat_copy(h, j):
        return to_blk(j, fsend.at[h, j], frecv.at[h, j], f_send.at[h, j], f_recv.at[h, j])

    def part_copy(h, k):
        rows_there = pl.ds(pl.multiple_of(rep_to(k) * chunk, chunk), chunk)
        return to_rep(k, rsend.at[h, rows_there], rrecv.at[h, k], r_send.at[h, k], r_recv.at[h, k])

    def grad_copy(h, k):
        here = grads[h].at[rep // per_panel, my_part]
        return to_rep(k, here, here, g_send.at[h, k], g_recv.at[h, k])

    def back_copy(h, j):
        return to_blk(j, bsend.at[h, j], brecv.at[h, j], b_send.at[h, j], b_recv.at[h, j])

    def fpart_copy(h, k):
        rows_there = pl.ds(pl.multiple_of(rep_to(k) * chunk, chunk), chunk)
        return to_rep(k, qsend.at[h, rows_there], qrecv.at[h, k], q_send.at[h, k], q_recv.at[h, k])

    def wpart_copy(j):
        there = pl.ds(pl.multiple_of(blk_to(j) * wchunk, wchunk), wchunk)
        return to_blk(j, wlocal.at[there], wrecv.at[j], w1_send.at[j], w1_recv.at[j])

    def wrep_copy(k):
        return to_rep(k, wrep.at[rep], wrep.at[rep], w2_send.at[k], w2_recv.at[k])

    wmine = pl.ds(pl.multiple_of(blk * wchunk, wchunk), wchunk)

    def wall_copy(j):
        return to_blk(j, wgrad.at[wmine], wgrad.at[wmine], w3_send.at[j], w3_recv.at[j])

    mine = pl.ds(pl.multiple_of(rep * chunk, chunk), chunk)

    barrier = pltpu.get_barrier_semaphore()

    def greet_blk(j):
        pl.semaphore_signal(barrier, inc=1, device_id={"blk": blk_to(j)}, device_id_type=MESH)

    def greet_rep(k):
        pl.semaphore_signal(barrier, inc=1, device_id={"rep": rep_to(k)}, device_id_type=MESH)

    each(n_blk, greet_blk)
    each(n_rep, greet_rep)
    pl.semaphore_wait(barrier, n_blk + n_rep - 2)

    far_first(lambda j: idx_copy(j).start())

    def in_use(owner, s):
        return s < count[0, 0, owner]

    def panel(p):
        return slice(p * tile, (p + 1) * tile)

    for s in range(slots):
        col = cols[blk, s]
        product = dot(tiles[blk, s], feat[col], 1, 0)
        for p in range(panels):
            keep = jnp.where((rows[blk, s] == p) & in_use(blk, s), 1.0, 0.0)
            for h in range(HALVES):
                piece = keep * product[:, h * width:(h + 1) * width]
                acc[h, panel(p), :] = piece if s == 0 else acc[h, panel(p), :] + piece

    def take_idx(j):
        idx_copy(j).wait_recv()
        local = pltpu.make_async_copy(idx_vec.at[j], idx.at[j], idx_local.at[j])
        local.start()
        local.wait()

    each(n_blk, take_idx)

    for h in range(HALVES):
        def serve(j, h=h):
            for s in range(slots):
                col = idx[j, blk, s]
                fsend[h, opposite(j), s] = feat[col][:, h * width:(h + 1) * width]
            feat_copy(h, opposite(j)).start()

        def opposite(j):
            return ((chips - j // 2) % chips) * 2 + j % 2

        far_first(serve)

    for h in range(HALVES):
        def absorb(j, h=h):
            feat_copy(h, j).wait_recv()
            owner = blk_from(j)
            products = [dot(tiles[owner, s], frecv[h, j, s], 1, 0) for s in range(slots)]
            for p in range(panels):
                total = acc[h, panel(p), :]
                for s in range(slots):
                    keep = jnp.where((rows[owner, s] == p) & in_use(owner, s), 1.0, 0.0)
                    total = total + keep * products[s]
                acc[h, panel(p), :] = total

        each(n_blk, absorb)
        rsend[h] = acc[h].astype(BF16)
        each(n_rep, lambda k, h=h: part_copy(h, k).start())

    for h in range(HALVES):
        each(n_rep, lambda k, h=h: part_copy(h, k).wait_recv())
        total = acc[h, mine, :]
        for k in range(1, n_rep):
            total = total + rrecv[h, k].astype(F32)
        agg[:, h * width:(h + 1) * width] = total.astype(BF16)

    pre_act = dot(agg[...], weight[...], 1, 0)
    bent = jnp.tanh(GELU_SCALE * (pre_act + GELU_CUBIC * pre_act * pre_act * pre_act))
    out[...] = (0.5 * pre_act * (1.0 + bent)).astype(BF16)
    slope = 0.5 * (1.0 + bent) + 0.5 * pre_act * (1.0 - bent * bent) * GELU_SCALE * (
        1.0 + 3.0 * GELU_CUBIC * pre_act * pre_act
    )
    pre_grad = (cot[...].astype(F32) * slope).astype(BF16)
    agg_grad = dot(pre_grad, weight[...], 1, 1).astype(BF16)
    for h in range(HALVES):
        grads[h][rep // per_panel, my_part, :] = agg_grad[:, h * width:(h + 1) * width]
        each(n_rep, lambda k, h=h: grad_copy(h, k).start())

    wlocal[...] = dot(agg[...], pre_grad, 0, 0)
    far_first(lambda j: wpart_copy(j).start())

    def back_product(h, owner, s):
        return dot(tiles[owner, s], grads[h][rows[owner, s]], 0, 0)

    for h in range(HALVES):
        each(n_rep, lambda k, h=h: grad_copy(h, k).wait_recv())

        def give(j, h=h):
            owner = blk_to(j)
            for s in range(slots):
                keep = jnp.where(in_use(owner, s), 1.0, 0.0)
                bsend[h, j, s] = (keep * back_product(h, owner, s)).astype(BF16)
            back_copy(h, j).start()

        far_first(give)

    wtotal = wlocal[wmine, :]
    each(n_blk, lambda j: wpart_copy(j).wait_recv())
    for j in range(1, n_blk):
        wtotal = wtotal + wrecv[j]
    wrep[rep] = wtotal
    each(n_rep, lambda k: wrep_copy(k).start())

    for h in range(HALVES):
        for s in range(slots):
            product = back_product(h, blk, s)
            for p in range(panels):
                keep = jnp.where((cols[blk, s] == p) & in_use(blk, s), 1.0, 0.0)
                piece = keep * product
                facc[h, panel(p), :] = piece if s == 0 else facc[h, panel(p), :] + piece

    for h in range(HALVES):
        def collect(j, h=h):
            back_copy(h, j).wait_recv()
            for p in range(panels):
                total = facc[h, panel(p), :]
                for s in range(slots):
                    keep = jnp.where(idx[j, blk, s] == p, 1.0, 0.0)
                    total = total + keep * brecv[h, j, s].astype(F32)
                facc[h, panel(p), :] = total

        each(n_blk, collect)
        qsend[h] = facc[h].astype(BF16)
        each(n_rep, lambda k, h=h: fpart_copy(h, k).start())
        if h == 0:
            each(n_rep, lambda k: wrep_copy(k).wait_recv())
            wtotal = wrep[0]
            for k in range(1, n_rep):
                wtotal = wtotal + wrep[k]
            wgrad[wmine, :] = wtotal
            far_first(lambda j: wall_copy(j).start())

    for h in range(HALVES):
        each(n_rep, lambda k, h=h: fpart_copy(h, k).wait_recv())
        total = facc[h, mine, :]
        for k in range(1, n_rep):
            total = total + qrecv[h, k].astype(F32)
        fgrad[:, h * width:(h + 1) * width] = total.astype(BF16)

    def finish_blk(j):
        wall_copy(j).wait_recv()
        idx_copy(j).wait_send()
        wpart_copy(j).wait_send()
        wall_copy(j).wait_send()
        for h in range(HALVES):
            feat_copy(h, j).wait_send()
            back_copy(h, j).wait_send()

    def finish_rep(k):
        wrep_copy(k).wait_send()
        for h in range(HALVES):
            part_copy(h, k).wait_send()
            grad_copy(h, k).wait_send()
            fpart_copy(h, k).wait_send()

    each(n_blk, finish_blk)
    each(n_rep, finish_rep)


def on_device(features, weight, cotangent, tiles, tile_rows, tile_cols, tile_count):
    n_blk, n_rep = lax.axis_size("blk"), lax.axis_size("rep")
    nodes, hidden = features.shape
    slots, tile = tiles.shape[3], tiles.shape[-1]
    width, chunk, wchunk = hidden // HALVES, nodes // n_rep, hidden // n_blk
    cols = tile_cols.reshape(n_blk, slots)
    vmem = pl.BlockSpec(memory_space=pltpu.VMEM)
    smem = pl.BlockSpec(memory_space=pltpu.SMEM)
    dma = pltpu.SemaphoreType.DMA
    by_blk, by_rep = dma((HALVES, n_blk)), dma((HALVES, n_rep))
    return pl.pallas_call(
        functools.partial(layer_kernel, n_blk, n_rep),
        out_shape=(
            jax.ShapeDtypeStruct((chunk, hidden), BF16),
            jax.ShapeDtypeStruct((chunk, hidden), BF16),
            jax.ShapeDtypeStruct((hidden, hidden), F32),
        ),
        in_specs=[vmem, vmem, vmem, vmem, smem, smem, smem, vmem],
        out_specs=(vmem, vmem, vmem),
        scratch_shapes=[
            pltpu.VMEM((n_blk, n_blk, slots), jnp.int32),
            pltpu.SMEM((n_blk, n_blk, slots), jnp.int32),
            pltpu.VMEM((HALVES, n_blk, slots, tile, width), BF16),
            pltpu.VMEM((HALVES, n_blk, slots, tile, width), BF16),
            pltpu.VMEM((HALVES, nodes, width), F32),
            pltpu.VMEM((HALVES, nodes, width), BF16),
            pltpu.VMEM((HALVES, n_rep, chunk, width), BF16),
            pltpu.VMEM((chunk, hidden), BF16),
            pltpu.VMEM((nodes // tile, tile, width), BF16),
            pltpu.VMEM((nodes // tile, tile, width), BF16),
            pltpu.VMEM((HALVES, n_blk, slots, tile, width), BF16),
            pltpu.VMEM((HALVES, n_blk, slots, tile, width), BF16),
            pltpu.VMEM((HALVES, nodes, width), F32),
            pltpu.VMEM((HALVES, nodes, width), BF16),
            pltpu.VMEM((HALVES, n_rep, chunk, width), BF16),
            pltpu.VMEM((hidden, hidden), F32),
            pltpu.VMEM((n_blk, wchunk, hidden), F32),
            pltpu.VMEM((n_rep, wchunk, hidden), F32),
            dma((n_blk,)), dma((n_blk,)), dma((n_blk,)),
            by_blk, by_blk, by_rep, by_rep, by_rep, by_rep,
            by_blk, by_blk, by_rep, by_rep,
            dma((n_blk,)), dma((n_blk,)), dma((n_rep,)), dma((n_rep,)), dma((n_blk,)), dma((n_blk,)),
        ],
        compiler_params=pltpu.CompilerParams(
            collective_id=0, has_side_effects=True, vmem_limit_bytes=56 * 1024 * 1024
        ),
    )(
        features.reshape(nodes // tile, tile, hidden), weight, cotangent, tiles.reshape(n_blk, slots, tile, tile),
        tile_rows.reshape(n_blk, slots), cols, tile_count, cols,
    )


def solution(mesh):
    in_specs = (
        P(("groups", "blk"), None),
        P(),
        P(("groups", "blk", "rep"), None),
        P(("groups", "blk"), "rep", None, None, None, None),
        P(("groups", "blk"), "rep", None, None),
        P(("groups", "blk"), "rep", None, None),
        P(("groups", "blk"), "rep", None),
    )
    out_specs = (
        P(("groups", "blk", "rep"), None),
        P(("groups", "blk", "rep"), None),
        P("groups", None),
    )
    return jax.shard_map(
        on_device, mesh=mesh, in_specs=in_specs, out_specs=out_specs, check_vma=False
    )
```

```python
import functools

import jax
import jax.numpy as jnp
from jax import lax
from jax.experimental import pallas as pl
from jax.experimental.pallas import tpu as pltpu
from jax.sharding import PartitionSpec as P

MESH = pl.DeviceIdType.MESH
HALVES = 2
F32 = jnp.float32
BF16 = jnp.bfloat16
GELU_SCALE = 0.7978845608028654
GELU_CUBIC = 0.044715


def dot(left, right, left_dim, right_dim):
    return lax.dot_general(
        left, right, (((left_dim,), (right_dim,)), ((), ())), preferred_element_type=F32
    )


def layer_kernel(
    n_blk, n_rep,
    feat, weight, cot, tiles, rows, cols, count, cols_vec,
    out, fgrad, wgrad,
    idx_vec, idx, fsend, frecv, acc, rsend, rrecv, agg, grad0, grad1,
    bsend, brecv, facc, qsend, qrecv, wlocal, wrecv, wrep,
    idx_send, idx_recv, idx_local, f_send, f_recv, r_send, r_recv, g_send, g_recv,
    b_send, b_recv, q_send, q_recv, w1_send, w1_recv, w2_send, w2_recv, w3_send, w3_recv,
):
    tile = tiles.shape[-1]
    slots = tiles.shape[1]
    panels = feat.shape[0]
    hidden = feat.shape[2]
    width = hidden // HALVES
    chunk = panels * tile // n_rep
    per_panel = tile // chunk
    wchunk = hidden // n_blk
    chips = n_blk // 2
    blk = lax.axis_index("blk")
    rep = lax.axis_index("rep")
    chip, core = blk // 2, blk % 2
    grads = (grad0, grad1)

    def blk_to(j):
        return ((chip + j // 2) % chips) * 2 + (core + j) % 2

    def blk_from(j):
        return ((chip + chips - j // 2) % chips) * 2 + (core + j) % 2

    def rep_to(k):
        return (rep + k) % n_rep

    def to_blk(j, src, dst, send_sem, recv_sem):
        return pltpu.make_async_remote_copy(
            src_ref=src, dst_ref=dst, send_sem=send_sem, recv_sem=recv_sem,
            device_id={"blk": blk_to(j)}, device_id_type=MESH,
        )

    def to_rep(k, src, dst, send_sem, recv_sem):
        return pltpu.make_async_remote_copy(
            src_ref=src, dst_ref=dst, send_sem=send_sem, recv_sem=recv_sem,
            device_id={"rep": rep_to(k)}, device_id_type=MESH,
        )

    def each(total, body):
        def step(at, carry):
            body(at)
            return carry
        if total <= 4:
            for at in range(1, total):
                body(at)
        else:
            lax.fori_loop(1, total, step, 0)

    def far_first(body):
        if n_blk <= 4:
            for j in list(range(2, n_blk)) + [1]:
                body(j)
        else:
            each(n_blk, body)

    my_part = pl.ds(pl.multiple_of((rep % per_panel) * chunk, chunk), chunk)

    def idx_copy(j):
        return to_blk(j, cols_vec, idx_vec.at[j], idx_send.at[j], idx_recv.at[j])

    def feat_copy(h, j):
        return to_blk(j, fsend.at[h, j], frecv.at[h, j], f_send.at[h, j], f_recv.at[h, j])

    def part_copy(h, k):
        rows_there = pl.ds(pl.multiple_of(rep_to(k) * chunk, chunk), chunk)
        return to_rep(k, rsend.at[h, rows_there], rrecv.at[h, k], r_send.at[h, k], r_recv.at[h, k])

    def grad_copy(h, k):
        here = grads[h].at[rep // per_panel, my_part]
        return to_rep(k, here, here, g_send.at[h, k], g_recv.at[h, k])

    def back_copy(h, j):
        return to_blk(j, bsend.at[h, j], brecv.at[h, j], b_send.at[h, j], b_recv.at[h, j])

    def fpart_copy(h, k):
        rows_there = pl.ds(pl.multiple_of(rep_to(k) * chunk, chunk), chunk)
        return to_rep(k, qsend.at[h, rows_there], qrecv.at[h, k], q_send.at[h, k], q_recv.at[h, k])

    def wpart_copy(j):
        there = pl.ds(pl.multiple_of(blk_to(j) * wchunk, wchunk), wchunk)
        return to_blk(j, wlocal.at[there], wrecv.at[j], w1_send.at[j], w1_recv.at[j])

    def wrep_copy(k):
        return to_rep(k, wrep.at[rep], wrep.at[rep], w2_send.at[k], w2_recv.at[k])

    wmine = pl.ds(pl.multiple_of(blk * wchunk, wchunk), wchunk)

    def wall_copy(j):
        return to_blk(j, wgrad.at[wmine], wgrad.at[wmine], w3_send.at[j], w3_recv.at[j])

    mine = pl.ds(pl.multiple_of(rep * chunk, chunk), chunk)

    barrier = pltpu.get_barrier_semaphore()

    def greet_blk(j):
        pl.semaphore_signal(barrier, inc=1, device_id={"blk": blk_to(j)}, device_id_type=MESH)

    def greet_rep(k):
        pl.semaphore_signal(barrier, inc=1, device_id={"rep": rep_to(k)}, device_id_type=MESH)

    each(n_blk, greet_blk)
    each(n_rep, greet_rep)
    pl.semaphore_wait(barrier, n_blk + n_rep - 2)

    far_first(lambda j: idx_copy(j).start())

    def in_use(owner, s):
        return s < count[0, 0, owner]

    def panel(p):
        return slice(p * tile, (p + 1) * tile)

    for s in range(slots):
        col = cols[s, blk]
        product = dot(tiles[blk, s], feat[col], 1, 0)
        for p in range(panels):
            keep = jnp.where((rows[s, blk] == p) & in_use(blk, s), 1.0, 0.0)
            for h in range(HALVES):
                piece = keep * product[:, h * width:(h + 1) * width]
                acc[h, panel(p), :] = piece if s == 0 else acc[h, panel(p), :] + piece

    def take_idx(j):
        idx_copy(j).wait_recv()
        local = pltpu.make_async_copy(idx_vec.at[j], idx.at[j], idx_local.at[j])
        local.start()
        local.wait()

    each(n_blk, take_idx)


    for h in range(HALVES):
        def serve(j, h=h):
            for s in range(slots):
                col = idx[j, s, blk]
                fsend[h, opposite(j), s] = feat[col][:, h * width:(h + 1) * width]
            feat_copy(h, opposite(j)).start()

        def opposite(j):
            return ((chips - j // 2) % chips) * 2 + j % 2

        far_first(serve)

    for h in range(HALVES):
        def absorb(j, h=h):
            feat_copy(h, j).wait_recv()
            owner = blk_from(j)
            products = [dot(tiles[owner, s], frecv[h, j, s], 1, 0) for s in range(slots)]
            for p in range(panels):
                total = acc[h, panel(p), :]
                for s in range(slots):
                    keep = jnp.where((rows[s, owner] == p) & in_use(owner, s), 1.0, 0.0)
                    total = total + keep * products[s]
                acc[h, panel(p), :] = total

        each(n_blk, absorb)
        rsend[h] = acc[h].astype(BF16)
        each(n_rep, lambda k, h=h: part_copy(h, k).start())

    for h in range(HALVES):
        each(n_rep, lambda k, h=h: part_copy(h, k).wait_recv())
        total = acc[h, mine, :]
        for k in range(1, n_rep):
            total = total + rrecv[h, k].astype(F32)
        agg[:, h * width:(h + 1) * width] = total.astype(BF16)

    pre_act = dot(agg[...], weight[...], 1, 0)
    bent = jnp.tanh(GELU_SCALE * (pre_act + GELU_CUBIC * pre_act * pre_act * pre_act))
    out[...] = (0.5 * pre_act * (1.0 + bent)).astype(BF16)
    slope = 0.5 * (1.0 + bent) + 0.5 * pre_act * (1.0 - bent * bent) * GELU_SCALE * (
        1.0 + 3.0 * GELU_CUBIC * pre_act * pre_act
    )
    pre_grad = (cot[...].astype(F32) * slope).astype(BF16)
    agg_grad = dot(pre_grad, weight[...], 1, 1).astype(BF16)
    for h in range(HALVES):
        grads[h][rep // per_panel, my_part, :] = agg_grad[:, h * width:(h + 1) * width]
        each(n_rep, lambda k, h=h: grad_copy(h, k).start())

    wlocal[...] = dot(agg[...], pre_grad, 0, 0)
    far_first(lambda j: wpart_copy(j).start())

    def back_product(h, owner, s):
        return dot(tiles[owner, s], grads[h][rows[s, owner]], 0, 0)

    for h in range(HALVES):
        each(n_rep, lambda k, h=h: grad_copy(h, k).wait_recv())

        def give(j, h=h):
            owner = blk_to(j)
            for s in range(slots):
                keep = jnp.where(in_use(owner, s), 1.0, 0.0)
                bsend[h, j, s] = (keep * back_product(h, owner, s)).astype(BF16)
            back_copy(h, j).start()

        far_first(give)

    wtotal = wlocal[wmine, :]
    each(n_blk, lambda j: wpart_copy(j).wait_recv())
    for j in range(1, n_blk):
        wtotal = wtotal + wrecv[j]
    wrep[rep] = wtotal
    each(n_rep, lambda k: wrep_copy(k).start())

    for h in range(HALVES):
        for s in range(slots):
            product = back_product(h, blk, s)
            for p in range(panels):
                keep = jnp.where((cols[s, blk] == p) & in_use(blk, s), 1.0, 0.0)
                piece = keep * product
                facc[h, panel(p), :] = piece if s == 0 else facc[h, panel(p), :] + piece

    for h in range(HALVES):
        def collect(j, h=h):
            back_copy(h, j).wait_recv()
            for p in range(panels):
                total = facc[h, panel(p), :]
                for s in range(slots):
                    keep = jnp.where(idx[j, s, blk] == p, 1.0, 0.0)
                    total = total + keep * brecv[h, j, s].astype(F32)
                facc[h, panel(p), :] = total

        each(n_blk, collect)
        qsend[h] = facc[h].astype(BF16)
        each(n_rep, lambda k, h=h: fpart_copy(h, k).start())
        if h == 0:
            each(n_rep, lambda k: wrep_copy(k).wait_recv())
            wtotal = wrep[0]
            for k in range(1, n_rep):
                wtotal = wtotal + wrep[k]
            wgrad[wmine, :] = wtotal
            far_first(lambda j: wall_copy(j).start())

    for h in range(HALVES):
        each(n_rep, lambda k, h=h: fpart_copy(h, k).wait_recv())
        total = facc[h, mine, :]
        for k in range(1, n_rep):
            total = total + qrecv[h, k].astype(F32)
        fgrad[:, h * width:(h + 1) * width] = total.astype(BF16)

    def finish_blk(j):
        wall_copy(j).wait_recv()
        idx_copy(j).wait_send()
        wpart_copy(j).wait_send()
        wall_copy(j).wait_send()
        for h in range(HALVES):
            feat_copy(h, j).wait_send()
            back_copy(h, j).wait_send()

    def finish_rep(k):
        wrep_copy(k).wait_send()
        for h in range(HALVES):
            part_copy(h, k).wait_send()
            grad_copy(h, k).wait_send()
            fpart_copy(h, k).wait_send()

    each(n_blk, finish_blk)
    each(n_rep, finish_rep)


def hand_over(out_in, fgrad_in, wgrad_in, out, fgrad, wgrad):
    out[...] = out_in[...]
    fgrad[...] = fgrad_in[...]
    wgrad[...] = wgrad_in[...]


def on_device(features, weight, cotangent, tiles, tile_rows, tile_cols, tile_count):
    n_blk, n_rep = lax.axis_size("blk"), lax.axis_size("rep")
    nodes, hidden = features.shape
    slots, tile = tiles.shape[3], tiles.shape[-1]
    width, chunk, wchunk = hidden // HALVES, nodes // n_rep, hidden // n_blk
    cols = tile_cols[0, 0].T
    vmem = pl.BlockSpec(memory_space=pltpu.VMEM)
    smem = pl.BlockSpec(memory_space=pltpu.SMEM)
    dma = pltpu.SemaphoreType.DMA
    by_blk, by_rep = dma((HALVES, n_blk)), dma((HALVES, n_rep))
    results = pl.pallas_call(
        functools.partial(layer_kernel, n_blk, n_rep),
        out_shape=(
            jax.ShapeDtypeStruct((chunk, hidden), BF16),
            jax.ShapeDtypeStruct((chunk, hidden), BF16),
            jax.ShapeDtypeStruct((hidden, hidden), F32),
        ),
        in_specs=[vmem, vmem, vmem, vmem, smem, smem, smem, vmem],
        out_specs=(vmem, vmem, vmem),
        scratch_shapes=[
            pltpu.VMEM((n_blk, slots, n_blk), jnp.int32),
            pltpu.SMEM((n_blk, slots, n_blk), jnp.int32),
            pltpu.VMEM((HALVES, n_blk, slots, tile, width), BF16),
            pltpu.VMEM((HALVES, n_blk, slots, tile, width), BF16),
            pltpu.VMEM((HALVES, nodes, width), F32),
            pltpu.VMEM((HALVES, nodes, width), BF16),
            pltpu.VMEM((HALVES, n_rep, chunk, width), BF16),
            pltpu.VMEM((chunk, hidden), BF16),
            pltpu.VMEM((nodes // tile, tile, width), BF16),
            pltpu.VMEM((nodes // tile, tile, width), BF16),
            pltpu.VMEM((HALVES, n_blk, slots, tile, width), BF16),
            pltpu.VMEM((HALVES, n_blk, slots, tile, width), BF16),
            pltpu.VMEM((HALVES, nodes, width), F32),
            pltpu.VMEM((HALVES, nodes, width), BF16),
            pltpu.VMEM((HALVES, n_rep, chunk, width), BF16),
            pltpu.VMEM((hidden, hidden), F32),
            pltpu.VMEM((n_blk, wchunk, hidden), F32),
            pltpu.VMEM((n_rep, wchunk, hidden), F32),
            dma((n_blk,)), dma((n_blk,)), dma((n_blk,)),
            by_blk, by_blk, by_rep, by_rep, by_rep, by_rep,
            by_blk, by_blk, by_rep, by_rep,
            dma((n_blk,)), dma((n_blk,)), dma((n_rep,)), dma((n_rep,)), dma((n_blk,)), dma((n_blk,)),
        ],
        compiler_params=pltpu.CompilerParams(
            collective_id=0, has_side_effects=True, vmem_limit_bytes=56 * 1024 * 1024
        ),
    )(
        features.reshape(nodes // tile, tile, hidden), weight, cotangent, tiles.reshape(n_blk, slots, tile, tile),
        tile_rows[0, 0].T, cols, tile_count, cols,
    )
    return pl.pallas_call(
        hand_over,
        out_shape=tuple(jax.ShapeDtypeStruct(r.shape, r.dtype) for r in results),
        in_specs=[vmem] * 3,
        out_specs=(vmem, vmem, vmem),
    )(*results)


def solution(mesh):
    in_specs = (
        P(("groups", "blk"), None),
        P(),
        P(("groups", "blk", "rep"), None),
        P(("groups", "blk"), "rep", None, None, None, None),
        P(("groups", "blk"), "rep", None, None),
        P(("groups", "blk"), "rep", None, None),
        P(("groups", "blk"), "rep", None),
    )
    out_specs = (
        P(("groups", "blk", "rep"), None),
        P(("groups", "blk", "rep"), None),
        P("groups", None),
    )
    return jax.shard_map(
        on_device, mesh=mesh, in_specs=in_specs, out_specs=out_specs, check_vma=False
    )
```

```python
import functools

import jax
import jax.numpy as jnp
from jax import lax
from jax.experimental import pallas as pl
from jax.experimental.pallas import tpu as pltpu
from jax.sharding import PartitionSpec as P

MESH = pl.DeviceIdType.MESH
HALVES = 2
F32 = jnp.float32
BF16 = jnp.bfloat16
GELU_SCALE = 0.7978845608028654
GELU_CUBIC = 0.044715


def dot(left, right, left_dim, right_dim):
    return lax.dot_general(
        left, right, (((left_dim,), (right_dim,)), ((), ())), preferred_element_type=F32
    )


def layer_kernel(
    n_blk, n_rep,
    feat_in, weight_in, cot_in, tiles_in, rows, cols, count, cols_vec,
    out, fgrad, wgrad,
    feat, weight, cot, tiles, load, far, idx_vec, idx, acc, rsend, rrecv, agg, grad0, grad1,
    bsend, brecv, facc, qsend, qrecv, wlocal, wrecv, wrep,
    idx_send, idx_recv, idx_local, f_send, f_recv, r_send, r_recv, g_send, g_recv,
    b_send, b_recv, q_send, q_recv, w1_send, w1_recv, w2_send, w2_recv, w3_send, w3_recv,
):
    tile = tiles.shape[-1]
    slots = tiles.shape[1]
    panels = feat.shape[0]
    hidden = feat.shape[2]
    width = hidden // HALVES
    chunk = panels * tile // n_rep
    per_panel = tile // chunk
    wchunk = hidden // n_blk
    chips = n_blk // 2
    blk = lax.axis_index("blk")
    rep = lax.axis_index("rep")
    chip, core = blk // 2, blk % 2
    grads = (grad0, grad1)

    def blk_to(j):
        return ((chip + j // 2) % chips) * 2 + (core + j) % 2

    def blk_from(j):
        return ((chip + chips - j // 2) % chips) * 2 + (core + j) % 2

    def rep_to(k):
        return (rep + k) % n_rep

    def to_blk(j, src, dst, send_sem, recv_sem):
        return pltpu.make_async_remote_copy(
            src_ref=src, dst_ref=dst, send_sem=send_sem, recv_sem=recv_sem,
            device_id={"blk": blk_to(j)}, device_id_type=MESH,
        )

    def to_rep(k, src, dst, send_sem, recv_sem):
        return pltpu.make_async_remote_copy(
            src_ref=src, dst_ref=dst, send_sem=send_sem, recv_sem=recv_sem,
            device_id={"rep": rep_to(k)}, device_id_type=MESH,
        )

    def each(total, body):
        def step(at, carry):
            body(at)
            return carry
        if total <= 4:
            for at in range(1, total):
                body(at)
        else:
            lax.fori_loop(1, total, step, 0)

    def far_first(body):
        if n_blk <= 4:
            for j in list(range(2, n_blk)) + [1]:
                body(j)
        else:
            each(n_blk, body)

    my_part = pl.ds(pl.multiple_of((rep % per_panel) * chunk, chunk), chunk)

    def idx_copy(j):
        return to_blk(j, cols_vec, idx_vec.at[j], idx_send.at[j], idx_recv.at[j])

    def feat_copy(h, j):
        half = feat.at[:, :, h * width:(h + 1) * width]
        return to_blk(j, half, far[h][j - 1], f_send.at[h, j], f_recv.at[h, j])

    def pass_on(h, j):
        return to_blk(1, far[h][j - 1], far[h][j], f_send.at[h, j + 1], f_recv.at[h, j + 1])

    def part_copy(h, k):
        rows_there = pl.ds(pl.multiple_of(rep_to(k) * chunk, chunk), chunk)
        return to_rep(k, rsend.at[h, rows_there], rrecv.at[h, k], r_send.at[h, k], r_recv.at[h, k])

    def grad_copy(h, k):
        here = grads[h].at[rep // per_panel, my_part]
        return to_rep(k, here, here, g_send.at[h, k], g_recv.at[h, k])

    def back_copy(h, j):
        return to_blk(j, bsend.at[h, j], brecv.at[h, j], b_send.at[h, j], b_recv.at[h, j])

    def fpart_copy(h, k):
        rows_there = pl.ds(pl.multiple_of(rep_to(k) * chunk, chunk), chunk)
        return to_rep(k, qsend.at[h, rows_there], qrecv.at[h, k], q_send.at[h, k], q_recv.at[h, k])

    def wpart_copy(j):
        there = pl.ds(pl.multiple_of(blk_to(j) * wchunk, wchunk), wchunk)
        return to_blk(j, wlocal.at[there], wrecv.at[j], w1_send.at[j], w1_recv.at[j])

    def wrep_copy(k):
        return to_rep(k, wrep.at[rep], wrep.at[rep], w2_send.at[k], w2_recv.at[k])

    wmine = pl.ds(pl.multiple_of(blk * wchunk, wchunk), wchunk)

    def wall_copy(j):
        return to_blk(j, wgrad.at[wmine], wgrad.at[wmine], w3_send.at[j], w3_recv.at[j])

    mine = pl.ds(pl.multiple_of(rep * chunk, chunk), chunk)

    loads = [
        pltpu.make_async_copy(src, dst, load.at[at])
        for at, (src, dst) in enumerate(
            ((feat_in, feat), (tiles_in, tiles), (weight_in, weight), (cot_in, cot))
        )
    ]
    for copy in loads:
        copy.start()

    barrier = pltpu.get_barrier_semaphore()

    def greet_blk(j):
        pl.semaphore_signal(barrier, inc=1, device_id={"blk": blk_to(j)}, device_id_type=MESH)

    def greet_rep(k):
        pl.semaphore_signal(barrier, inc=1, device_id={"rep": rep_to(k)}, device_id_type=MESH)

    each(n_blk, greet_blk)
    each(n_rep, greet_rep)
    pl.semaphore_wait(barrier, n_blk + n_rep - 2)

    loads[0].wait()
    for h in range(HALVES):
        for j in list(range(2, n_blk, 2)) + [1]:
            feat_copy(h, j).start()
    far_first(lambda j: idx_copy(j).start())
    for copy in loads[1:]:
        copy.wait()

    def in_use(owner, s):
        return s < count[0, 0, owner]

    def panel(p):
        return slice(p * tile, (p + 1) * tile)

    for s in range(slots):
        col = cols[s, blk]
        product = dot(tiles[blk, s], feat[col], 1, 0)
        for p in range(panels):
            keep = jnp.where((rows[s, blk] == p) & in_use(blk, s), 1.0, 0.0)
            for h in range(HALVES):
                piece = keep * product[:, h * width:(h + 1) * width]
                acc[h, panel(p), :] = piece if s == 0 else acc[h, panel(p), :] + piece

    for h in range(HALVES):
        def absorb(j, h=h):
            owner = blk_from(j)
            products = [dot(tiles[owner, s], far[h][j - 1][cols[s, owner]], 1, 0) for s in range(slots)]
            for p in range(panels):
                total = acc[h, panel(p), :]
                for s in range(slots):
                    keep = jnp.where((rows[s, owner] == p) & in_use(owner, s), 1.0, 0.0)
                    total = total + keep * products[s]
                acc[h, panel(p), :] = total

        feat_copy(h, 1).wait_recv()
        absorb(1)
        for j in range(2, n_blk, 2):
            feat_copy(h, j).wait_recv()
            pass_on(h, j).start()
            absorb(j)
        for j in range(2, n_blk, 2):
            pass_on(h, j).wait_recv()
            absorb(j + 1)
        rsend[h] = acc[h].astype(BF16)
        each(n_rep, lambda k, h=h: part_copy(h, k).start())

    for h in range(HALVES):
        each(n_rep, lambda k, h=h: part_copy(h, k).wait_recv())
        total = acc[h, mine, :]
        for k in range(1, n_rep):
            total = total + rrecv[h, k].astype(F32)
        agg[:, h * width:(h + 1) * width] = total.astype(BF16)

    pre_act = dot(agg[...], weight[...], 1, 0)
    bent = jnp.tanh(GELU_SCALE * (pre_act + GELU_CUBIC * pre_act * pre_act * pre_act))
    out[...] = (0.5 * pre_act * (1.0 + bent)).astype(BF16)
    slope = 0.5 * (1.0 + bent) + 0.5 * pre_act * (1.0 - bent * bent) * GELU_SCALE * (
        1.0 + 3.0 * GELU_CUBIC * pre_act * pre_act
    )
    pre_grad = (cot[...].astype(F32) * slope).astype(BF16)
    agg_grad = dot(pre_grad, weight[...], 1, 1).astype(BF16)
    for h in range(HALVES):
        grads[h][rep // per_panel, my_part, :] = agg_grad[:, h * width:(h + 1) * width]
        each(n_rep, lambda k, h=h: grad_copy(h, k).start())

    wlocal[...] = dot(agg[...], pre_grad, 0, 0)
    far_first(lambda j: wpart_copy(j).start())

    def take_idx(j):
        idx_copy(j).wait_recv()
        local = pltpu.make_async_copy(idx_vec.at[j], idx.at[j], idx_local.at[j])
        local.start()
        local.wait()

    each(n_blk, take_idx)

    def back_product(h, owner, s):
        return dot(tiles[owner, s], grads[h][rows[s, owner]], 0, 0)

    for h in range(HALVES):
        each(n_rep, lambda k, h=h: grad_copy(h, k).wait_recv())

        def give(j, h=h):
            owner = blk_to(j)
            for s in range(slots):
                keep = jnp.where(in_use(owner, s), 1.0, 0.0)
                bsend[h, j, s] = (keep * back_product(h, owner, s)).astype(BF16)
            back_copy(h, j).start()

        far_first(give)
        if h == 0:
            wtotal = wlocal[wmine, :]
            each(n_blk, lambda j: wpart_copy(j).wait_recv())
            for j in range(1, n_blk):
                wtotal = wtotal + wrecv[j]
            wrep[rep] = wtotal.astype(BF16)
            each(n_rep, lambda k: wrep_copy(k).start())

    for h in range(HALVES):
        for s in range(slots):
            product = back_product(h, blk, s)
            for p in range(panels):
                keep = jnp.where((cols[s, blk] == p) & in_use(blk, s), 1.0, 0.0)
                piece = keep * product
                facc[h, panel(p), :] = piece if s == 0 else facc[h, panel(p), :] + piece

    for h in range(HALVES):
        def collect(j, h=h):
            back_copy(h, j).wait_recv()
            for p in range(panels):
                total = facc[h, panel(p), :]
                for s in range(slots):
                    keep = jnp.where(idx[j, s, blk] == p, 1.0, 0.0)
                    total = total + keep * brecv[h, j, s].astype(F32)
                facc[h, panel(p), :] = total

        each(n_blk, collect)
        qsend[h] = facc[h].astype(BF16)
        each(n_rep, lambda k, h=h: fpart_copy(h, k).start())
        if h == 0:
            each(n_rep, lambda k: wrep_copy(k).wait_recv())
            wtotal = wrep[0].astype(F32)
            for k in range(1, n_rep):
                wtotal = wtotal + wrep[k].astype(F32)
            wgrad[wmine, :] = wtotal
            far_first(lambda j: wall_copy(j).start())

    for h in range(HALVES):
        each(n_rep, lambda k, h=h: fpart_copy(h, k).wait_recv())
        total = facc[h, mine, :]
        for k in range(1, n_rep):
            total = total + qrecv[h, k].astype(F32)
        fgrad[:, h * width:(h + 1) * width] = total.astype(BF16)

    def finish_blk(j):
        wall_copy(j).wait_recv()
        idx_copy(j).wait_send()
        wpart_copy(j).wait_send()
        wall_copy(j).wait_send()
        for h in range(HALVES):
            back_copy(h, j).wait_send()

    def finish_rep(k):
        wrep_copy(k).wait_send()
        for h in range(HALVES):
            part_copy(h, k).wait_send()
            grad_copy(h, k).wait_send()
            fpart_copy(h, k).wait_send()

    for h in range(HALVES):
        for j in list(range(2, n_blk, 2)) + [1]:
            feat_copy(h, j).wait_send()
        for j in range(2, n_blk, 2):
            pass_on(h, j).wait_send()
    each(n_blk, finish_blk)
    each(n_rep, finish_rep)


def hand_over(out_in, fgrad_in, wgrad_in, out, fgrad, wgrad):
    out[...] = out_in[...]
    fgrad[...] = fgrad_in[...]
    wgrad[...] = wgrad_in[...]


def on_device(features, weight, cotangent, tiles, tile_rows, tile_cols, tile_count):
    n_blk, n_rep = lax.axis_size("blk"), lax.axis_size("rep")
    nodes, hidden = features.shape
    slots, tile = tiles.shape[3], tiles.shape[-1]
    panels = nodes // tile
    width, chunk, wchunk = hidden // HALVES, nodes // n_rep, hidden // n_blk
    cols = tile_cols[0, 0].T
    vmem = pl.BlockSpec(memory_space=pltpu.VMEM)
    smem = pl.BlockSpec(memory_space=pltpu.SMEM)
    whole = pl.BlockSpec(memory_space=pl.ANY)
    dma = pltpu.SemaphoreType.DMA
    by_blk, by_rep = dma((HALVES, n_blk)), dma((HALVES, n_rep))
    results = pl.pallas_call(
        functools.partial(layer_kernel, n_blk, n_rep),
        out_shape=(
            jax.ShapeDtypeStruct((chunk, hidden), BF16),
            jax.ShapeDtypeStruct((chunk, hidden), BF16),
            jax.ShapeDtypeStruct((hidden, hidden), F32),
        ),
        in_specs=[whole, whole, whole, whole, smem, smem, smem, vmem],
        out_specs=(vmem, vmem, vmem),
        scratch_shapes=[
            pltpu.VMEM((panels, tile, hidden), BF16),
            pltpu.VMEM((hidden, hidden), BF16),
            pltpu.VMEM((chunk, hidden), BF16),
            pltpu.VMEM((n_blk, slots, tile, tile), BF16),
            dma((4,)),
            [[pltpu.VMEM((panels, tile, width), BF16)] * (n_blk - 1)] * HALVES,
            pltpu.VMEM((n_blk, slots, n_blk), jnp.int32),
            pltpu.SMEM((n_blk, slots, n_blk), jnp.int32),
            pltpu.VMEM((HALVES, nodes, width), F32),
            pltpu.VMEM((HALVES, nodes, width), BF16),
            pltpu.VMEM((HALVES, n_rep, chunk, width), BF16),
            pltpu.VMEM((chunk, hidden), BF16),
            pltpu.VMEM((nodes // tile, tile, width), BF16),
            pltpu.VMEM((nodes // tile, tile, width), BF16),
            pltpu.VMEM((HALVES, n_blk, slots, tile, width), BF16),
            pltpu.VMEM((HALVES, n_blk, slots, tile, width), BF16),
            pltpu.VMEM((HALVES, nodes, width), F32),
            pltpu.VMEM((HALVES, nodes, width), BF16),
            pltpu.VMEM((HALVES, n_rep, chunk, width), BF16),
            pltpu.VMEM((hidden, hidden), F32),
            pltpu.VMEM((n_blk, wchunk, hidden), F32),
            pltpu.VMEM((n_rep, wchunk, hidden), BF16),
            dma((n_blk,)), dma((n_blk,)), dma((n_blk,)),
            by_blk, by_blk, by_rep, by_rep, by_rep, by_rep,
            by_blk, by_blk, by_rep, by_rep,
            dma((n_blk,)), dma((n_blk,)), dma((n_rep,)), dma((n_rep,)), dma((n_blk,)), dma((n_blk,)),
        ],
        compiler_params=pltpu.CompilerParams(
            collective_id=0, has_side_effects=True, vmem_limit_bytes=56 * 1024 * 1024
        ),
    )(
        features.reshape(nodes // tile, tile, hidden), weight, cotangent, tiles.reshape(n_blk, slots, tile, tile),
        tile_rows[0, 0].T, cols, tile_count, cols,
    )
    return pl.pallas_call(
        hand_over,
        out_shape=tuple(jax.ShapeDtypeStruct(r.shape, r.dtype) for r in results),
        in_specs=[vmem] * 3,
        out_specs=(vmem, vmem, vmem),
    )(*results)


def solution(mesh):
    in_specs = (
        P(("groups", "blk"), None),
        P(),
        P(("groups", "blk", "rep"), None),
        P(("groups", "blk"), "rep", None, None, None, None),
        P(("groups", "blk"), "rep", None, None),
        P(("groups", "blk"), "rep", None, None),
        P(("groups", "blk"), "rep", None),
    )
    out_specs = (
        P(("groups", "blk", "rep"), None),
        P(("groups", "blk", "rep"), None),
        P("groups", None),
    )
    return jax.shard_map(
        on_device, mesh=mesh, in_specs=in_specs, out_specs=out_specs, check_vma=False
    )
```

```python
import functools

import jax
import jax.numpy as jnp
from jax import lax
from jax.experimental import pallas as pl
from jax.experimental.pallas import tpu as pltpu
from jax.sharding import PartitionSpec as P

MESH = pl.DeviceIdType.MESH
HALVES = 2
STRIPS = 1
F32 = jnp.float32
BF16 = jnp.bfloat16
GELU_SCALE = 0.7978845608028654
GELU_CUBIC = 0.044715


def dot(left, right, left_dim, right_dim):
    return lax.dot_general(
        left, right, (((left_dim,), (right_dim,)), ((), ())), preferred_element_type=F32
    )


def layer_kernel(
    n_blk, n_rep,
    feat_in, weight_in, cot_in, tiles_in, rows, cols, count, cols_vec,
    out, fgrad, wgrad,
    feat, weight, cot, tiles, load, far, idx_vec, idx, acc, rsend, rrecv, agg, pre_grad, grad0, grad1,
    bsend, brecv, facc, qsend, qrecv, wlocal, wrecv, wrep,
    idx_send, idx_recv, idx_local, f_send, f_recv, r_send, r_recv, g_send, g_recv,
    b_send, b_recv, q_send, q_recv, w1_send, w1_recv, w2_send, w2_recv, w3_send, w3_recv,
):
    tile = tiles.shape[-1]
    slots = tiles.shape[1]
    panels = feat.shape[0]
    hidden = feat.shape[2]
    width = hidden // HALVES
    chunk = panels * tile // n_rep
    per_panel = tile // chunk
    strip = chunk // STRIPS
    wchunk = hidden // n_blk
    chips = n_blk // 2
    blk = lax.axis_index("blk")
    rep = lax.axis_index("rep")
    chip, core = blk // 2, blk % 2
    grads = (grad0, grad1)

    def blk_to(j):
        return ((chip + j // 2) % chips) * 2 + (core + j) % 2

    def blk_from(j):
        return ((chip + chips - j // 2) % chips) * 2 + (core + j) % 2

    def rep_to(k):
        return (rep + k) % n_rep

    def to_blk(j, src, dst, send_sem, recv_sem):
        return pltpu.make_async_remote_copy(
            src_ref=src, dst_ref=dst, send_sem=send_sem, recv_sem=recv_sem,
            device_id={"blk": blk_to(j)}, device_id_type=MESH,
        )

    def to_rep(k, src, dst, send_sem, recv_sem):
        return pltpu.make_async_remote_copy(
            src_ref=src, dst_ref=dst, send_sem=send_sem, recv_sem=recv_sem,
            device_id={"rep": rep_to(k)}, device_id_type=MESH,
        )

    def each(total, body):
        def step(at, carry):
            body(at)
            return carry
        if total <= 4:
            for at in range(1, total):
                body(at)
        else:
            lax.fori_loop(1, total, step, 0)

    def far_first(body):
        if n_blk <= 4:
            for j in list(range(2, n_blk)) + [1]:
                body(j)
        else:
            each(n_blk, body)

    def idx_copy(j):
        return to_blk(j, cols_vec, idx_vec.at[j], idx_send.at[j], idx_recv.at[j])

    def feat_copy(h, j):
        half = feat.at[:, :, h * width:(h + 1) * width]
        return to_blk(j, half, far[h][j - 1], f_send.at[h, j], f_recv.at[h, j])

    def pass_on(h, j):
        return to_blk(1, far[h][j - 1], far[h][j], f_send.at[h, j + 1], f_recv.at[h, j + 1])

    def part_copy(h, k, t):
        rows_there = pl.ds(pl.multiple_of(rep_to(k) * chunk + t * strip, strip), strip)
        lands = rrecv.at[h, k, pl.ds(t * strip, strip)]
        return to_rep(k, rsend.at[h, rows_there], lands, r_send.at[h, k, t], r_recv.at[h, k, t])

    def my_strip(t):
        return pl.ds(pl.multiple_of((rep % per_panel) * chunk + t * strip, strip), strip)

    def grad_copy(h, k, t):
        here = grads[h].at[rep // per_panel, my_strip(t)]
        return to_rep(k, here, here, g_send.at[h, k, t], g_recv.at[h, k, t])

    def back_copy(h, j):
        return to_blk(j, bsend.at[h, j], brecv.at[h, j], b_send.at[h, j], b_recv.at[h, j])

    def fpart_copy(h, k):
        rows_there = pl.ds(pl.multiple_of(rep_to(k) * chunk, chunk), chunk)
        return to_rep(k, qsend.at[h, rows_there], qrecv.at[h, k], q_send.at[h, k], q_recv.at[h, k])

    def wpart_copy(j):
        there = pl.ds(pl.multiple_of(blk_to(j) * wchunk, wchunk), wchunk)
        return to_blk(j, wlocal.at[there], wrecv.at[j], w1_send.at[j], w1_recv.at[j])

    def wrep_copy(k):
        return to_rep(k, wrep.at[rep], wrep.at[rep], w2_send.at[k], w2_recv.at[k])

    wmine = pl.ds(pl.multiple_of(blk * wchunk, wchunk), wchunk)

    def wall_copy(j):
        return to_blk(j, wgrad.at[wmine], wgrad.at[wmine], w3_send.at[j], w3_recv.at[j])

    mine = pl.ds(pl.multiple_of(rep * chunk, chunk), chunk)

    loads = [
        pltpu.make_async_copy(src, dst, load.at[at])
        for at, (src, dst) in enumerate(
            ((feat_in, feat), (tiles_in, tiles), (weight_in, weight), (cot_in, cot))
        )
    ]
    for copy in loads:
        copy.start()

    barrier = pltpu.get_barrier_semaphore()

    def greet_blk(j):
        pl.semaphore_signal(barrier, inc=1, device_id={"blk": blk_to(j)}, device_id_type=MESH)

    def greet_rep(k):
        pl.semaphore_signal(barrier, inc=1, device_id={"rep": rep_to(k)}, device_id_type=MESH)

    each(n_blk, greet_blk)
    each(n_rep, greet_rep)
    pl.semaphore_wait(barrier, n_blk + n_rep - 2)

    loads[0].wait()
    for h in range(HALVES):
        for j in list(range(2, n_blk, 2)) + [1]:
            feat_copy(h, j).start()
    far_first(lambda j: idx_copy(j).start())
    for copy in loads[1:]:
        copy.wait()

    def in_use(owner, s):
        return s < count[0, 0, owner]

    def panel(p):
        return slice(p * tile, (p + 1) * tile)

    for s in range(slots):
        col = cols[s, blk]
        product = dot(tiles[blk, s], feat[col], 1, 0)
        for p in range(panels):
            keep = jnp.where((rows[s, blk] == p) & in_use(blk, s), 1.0, 0.0)
            for h in range(HALVES):
                piece = keep * product[:, h * width:(h + 1) * width]
                acc[h, panel(p), :] = piece if s == 0 else acc[h, panel(p), :] + piece

    for h in range(HALVES):
        def absorb(j, h=h):
            owner = blk_from(j)
            products = [dot(tiles[owner, s], far[h][j - 1][cols[s, owner]], 1, 0) for s in range(slots)]
            for p in range(panels):
                total = acc[h, panel(p), :]
                for s in range(slots):
                    keep = jnp.where((rows[s, owner] == p) & in_use(owner, s), 1.0, 0.0)
                    total = total + keep * products[s]
                acc[h, panel(p), :] = total

        feat_copy(h, 1).wait_recv()
        absorb(1)
        for j in range(2, n_blk, 2):
            feat_copy(h, j).wait_recv()
            pass_on(h, j).start()
            absorb(j)
        for j in range(2, n_blk, 2):
            pass_on(h, j).wait_recv()
            absorb(j + 1)
        rsend[h] = acc[h].astype(BF16)
        for t in range(STRIPS):
            each(n_rep, lambda k, h=h, t=t: part_copy(h, k, t).start())

    def gather_part(h, t):
        each(n_rep, lambda k: part_copy(h, k, t).wait_recv())
        here = slice(t * strip, (t + 1) * strip)
        total = acc[h, pl.ds(pl.multiple_of(rep * chunk + t * strip, strip), strip), :]
        for k in range(1, n_rep):
            total = total + rrecv[h, k, here].astype(F32)
        agg[here, h * width:(h + 1) * width] = total.astype(BF16)

    for h in range(HALVES - 1):
        for t in range(STRIPS):
            gather_part(h, t)

    for t in range(STRIPS):
        gather_part(HALVES - 1, t)
        here = slice(t * strip, (t + 1) * strip)
        pre_act = dot(agg[here, :], weight[...], 1, 0)
        bent = jnp.tanh(GELU_SCALE * (pre_act + GELU_CUBIC * pre_act * pre_act * pre_act))
        slope = 0.5 * (1.0 + bent) + 0.5 * pre_act * (1.0 - bent * bent) * GELU_SCALE * (
            1.0 + 3.0 * GELU_CUBIC * pre_act * pre_act
        )
        strip_grad = (cot[here, :].astype(F32) * slope).astype(BF16)
        agg_grad = dot(strip_grad, weight[...], 1, 1).astype(BF16)
        for h in range(HALVES):
            grads[h][rep // per_panel, my_strip(t), :] = agg_grad[:, h * width:(h + 1) * width]
        each(n_rep, lambda k, t=t: grad_copy(0, k, t).start())
        pre_grad[here, :] = strip_grad
        out[here, :] = (0.5 * pre_act * (1.0 + bent)).astype(BF16)
    for h in range(1, HALVES):
        for t in range(STRIPS):
            each(n_rep, lambda k, h=h, t=t: grad_copy(h, k, t).start())

    wlocal[...] = dot(agg[...], pre_grad[...], 0, 0)
    far_first(lambda j: wpart_copy(j).start())

    def take_idx(j):
        idx_copy(j).wait_recv()
        local = pltpu.make_async_copy(idx_vec.at[j], idx.at[j], idx_local.at[j])
        local.start()
        local.wait()

    each(n_blk, take_idx)

    def back_product(h, owner, s):
        return dot(tiles[owner, s], grads[h][rows[s, owner]], 0, 0)

    for h in range(HALVES):
        for t in range(STRIPS):
            each(n_rep, lambda k, h=h, t=t: grad_copy(h, k, t).wait_recv())

        def give(j, h=h):
            owner = blk_to(j)
            for s in range(slots):
                keep = jnp.where(in_use(owner, s), 1.0, 0.0)
                bsend[h, j, s] = (keep * back_product(h, owner, s)).astype(BF16)
            back_copy(h, j).start()

        far_first(give)
        if h == 0:
            wtotal = wlocal[wmine, :]
            each(n_blk, lambda j: wpart_copy(j).wait_recv())
            for j in range(1, n_blk):
                wtotal = wtotal + wrecv[j]
            wrep[rep] = wtotal.astype(BF16)
            each(n_rep, lambda k: wrep_copy(k).start())

    for h in range(HALVES):
        for s in range(slots):
            product = back_product(h, blk, s)
            for p in range(panels):
                keep = jnp.where((cols[s, blk] == p) & in_use(blk, s), 1.0, 0.0)
                piece = keep * product
                facc[h, panel(p), :] = piece if s == 0 else facc[h, panel(p), :] + piece

    for h in range(HALVES):
        def collect(j, h=h):
            back_copy(h, j).wait_recv()
            for p in range(panels):
                total = facc[h, panel(p), :]
                for s in range(slots):
                    keep = jnp.where(idx[j, s, blk] == p, 1.0, 0.0)
                    total = total + keep * brecv[h, j, s].astype(F32)
                facc[h, panel(p), :] = total

        each(n_blk, collect)
        qsend[h] = facc[h].astype(BF16)
        each(n_rep, lambda k, h=h: fpart_copy(h, k).start())
        if h == HALVES - 1:
            each(n_rep, lambda k: wrep_copy(k).wait_recv())
            wtotal = wrep[0].astype(F32)
            for k in range(1, n_rep):
                wtotal = wtotal + wrep[k].astype(F32)
            wgrad[wmine, :] = wtotal
            far_first(lambda j: wall_copy(j).start())

    for h in range(HALVES):
        each(n_rep, lambda k, h=h: fpart_copy(h, k).wait_recv())
        total = facc[h, mine, :]
        for k in range(1, n_rep):
            total = total + qrecv[h, k].astype(F32)
        fgrad[:, h * width:(h + 1) * width] = total.astype(BF16)

    def finish_blk(j):
        wall_copy(j).wait_recv()
        idx_copy(j).wait_send()
        wpart_copy(j).wait_send()
        wall_copy(j).wait_send()
        for h in range(HALVES):
            back_copy(h, j).wait_send()

    def finish_rep(k):
        wrep_copy(k).wait_send()
        for h in range(HALVES):
            for t in range(STRIPS):
                part_copy(h, k, t).wait_send()
                grad_copy(h, k, t).wait_send()
            fpart_copy(h, k).wait_send()

    for h in range(HALVES):
        for j in list(range(2, n_blk, 2)) + [1]:
            feat_copy(h, j).wait_send()
        for j in range(2, n_blk, 2):
            pass_on(h, j).wait_send()
    each(n_blk, finish_blk)
    each(n_rep, finish_rep)


def hand_over(out_in, fgrad_in, wgrad_in, out, fgrad, wgrad):
    out[...] = out_in[...]
    fgrad[...] = fgrad_in[...]
    wgrad[...] = wgrad_in[...]


def on_device(features, weight, cotangent, tiles, tile_rows, tile_cols, tile_count):
    n_blk, n_rep = lax.axis_size("blk"), lax.axis_size("rep")
    nodes, hidden = features.shape
    slots, tile = tiles.shape[3], tiles.shape[-1]
    panels = nodes // tile
    width, chunk, wchunk = hidden // HALVES, nodes // n_rep, hidden // n_blk
    cols = tile_cols[0, 0].T
    vmem = pl.BlockSpec(memory_space=pltpu.VMEM)
    smem = pl.BlockSpec(memory_space=pltpu.SMEM)
    whole = pl.BlockSpec(memory_space=pl.ANY)
    dma = pltpu.SemaphoreType.DMA
    by_blk, by_rep = dma((HALVES, n_blk)), dma((HALVES, n_rep))
    by_strip = dma((HALVES, n_rep, STRIPS))
    results = pl.pallas_call(
        functools.partial(layer_kernel, n_blk, n_rep),
        out_shape=(
            jax.ShapeDtypeStruct((chunk, hidden), BF16),
            jax.ShapeDtypeStruct((chunk, hidden), BF16),
            jax.ShapeDtypeStruct((hidden, hidden), F32),
        ),
        in_specs=[whole, whole, whole, whole, smem, smem, smem, vmem],
        out_specs=(vmem, vmem, vmem),
        scratch_shapes=[
            pltpu.VMEM((panels, tile, hidden), BF16),
            pltpu.VMEM((hidden, hidden), BF16),
            pltpu.VMEM((chunk, hidden), BF16),
            pltpu.VMEM((n_blk, slots, tile, tile), BF16),
            dma((4,)),
            [[pltpu.VMEM((panels, tile, width), BF16)] * (n_blk - 1)] * HALVES,
            pltpu.VMEM((n_blk, slots, n_blk), jnp.int32),
            pltpu.SMEM((n_blk, slots, n_blk), jnp.int32),
            pltpu.VMEM((HALVES, nodes, width), F32),
            pltpu.VMEM((HALVES, nodes, width), BF16),
            pltpu.VMEM((HALVES, n_rep, chunk, width), BF16),
            pltpu.VMEM((chunk, hidden), BF16),
            pltpu.VMEM((chunk, hidden), BF16),
            pltpu.VMEM((nodes // tile, tile, width), BF16),
            pltpu.VMEM((nodes // tile, tile, width), BF16),
            pltpu.VMEM((HALVES, n_blk, slots, tile, width), BF16),
            pltpu.VMEM((HALVES, n_blk, slots, tile, width), BF16),
            pltpu.VMEM((HALVES, nodes, width), F32),
            pltpu.VMEM((HALVES, nodes, width), BF16),
            pltpu.VMEM((HALVES, n_rep, chunk, width), BF16),
            pltpu.VMEM((hidden, hidden), F32),
            pltpu.VMEM((n_blk, wchunk, hidden), F32),
            pltpu.VMEM((n_rep, wchunk, hidden), BF16),
            dma((n_blk,)), dma((n_blk,)), dma((n_blk,)),
            by_blk, by_blk, by_strip, by_strip, by_strip, by_strip,
            by_blk, by_blk, by_rep, by_rep,
            dma((n_blk,)), dma((n_blk,)), dma((n_rep,)), dma((n_rep,)), dma((n_blk,)), dma((n_blk,)),
        ],
        compiler_params=pltpu.CompilerParams(
            collective_id=0, has_side_effects=True, vmem_limit_bytes=56 * 1024 * 1024
        ),
    )(
        features.reshape(nodes // tile, tile, hidden), weight, cotangent, tiles.reshape(n_blk, slots, tile, tile),
        tile_rows[0, 0].T, cols, tile_count, cols,
    )
    return pl.pallas_call(
        hand_over,
        out_shape=tuple(jax.ShapeDtypeStruct(r.shape, r.dtype) for r in results),
        in_specs=[vmem] * 3,
        out_specs=(vmem, vmem, vmem),
    )(*results)


def solution(mesh):
    in_specs = (
        P(("groups", "blk"), None),
        P(),
        P(("groups", "blk", "rep"), None),
        P(("groups", "blk"), "rep", None, None, None, None),
        P(("groups", "blk"), "rep", None, None),
        P(("groups", "blk"), "rep", None, None),
        P(("groups", "blk"), "rep", None),
    )
    out_specs = (
        P(("groups", "blk", "rep"), None),
        P(("groups", "blk", "rep"), None),
        P("groups", None),
    )
    return jax.shard_map(
        on_device, mesh=mesh, in_specs=in_specs, out_specs=out_specs, check_vma=False
    )
```
